256 devices in a mesh: clip: 16 (over z, core), seq: 16 (over x, y).
Axes of the slice: x: 4, y: 4, z: 8, core: 2. Of those that a mesh axis runs over, the one named last changes fastest.
Arguments:
- patches: bfloat16 [16, 10240, 1408], P('clip', 'seq'), may hold values from -6 to 6
- vis_index: int32 [16, 1024], P('clip'), may hold values from 0 to 10239, as said below
- enc_gain: float32 [1408], replicated, may hold values from 0.5 to 1.5
- w_qkv: bfloat16 [3, 1408, 1408], P(None, None, 'seq')
- w_out: bfloat16 [1408, 1408], P('seq'), may hold values from -2 to 2
- w_embed: bfloat16 [1408, 512], P(None, ('clip', 'seq')), may hold values from -0.15625 to 0.15625
- mask_token: bfloat16 [512], replicated, may hold values from -4 to 4
- pos_embed: bfloat16 [10240, 512], P('seq'), may hold values from -3 to 3
- dec_gain: float32 [512], replicated, may hold values from 0.5 to 1.5
- w_up: bfloat16 [512, 2048], P(None, ('clip', 'seq')), may hold values from -0.25 to 0.25
- w_down: bfloat16 [2048, 512], P(('clip', 'seq')), may hold values from -0.125 to 0.125
- w_pixel: bfloat16 [512, 1176], replicated, may hold values from -0.25 to 0.25
- target: bfloat16 [16, 10240, 1176], P('clip', 'seq'), may hold values from -6 to 6
Outputs:
- decoded: bfloat16 [16, 10240, 512], P('clip', 'seq')
- grad_pixel: float32 [16, 512, 1176], P('clip', 'seq')
The draws below stay inside these ranges and needn't reach their ends.
Inputs may be any that keep to these rules, and one draw needn't show every extreme that they name: `vis_index`: strictly ascending within a clip. Among the 640 consecutive positions of any one index of seq at most 128 are visible, and in every clip some index holds exactly 128.
All inputs are finite; a program needn't handle non-finite values.
Results may differ from the reference program's by a relative error of at most 0.022.
The reference program's roundings to bfloat16 on the way count: a program that leaves them out, or rounds other values in their place, can miss the bound.
Values may be sent and summed in bfloat16 or wider, within the bound.
A program may use at most 64 MiB of HBM per device.

```python
import jax
import jax.numpy as jnp
from jax import lax

D = 1408
H = 16
HEAD = 88
DEC = 512
HID = 2048
PIX = 1176
TOK_DEV = 640
CAP = 128
VIS = 1024
TOKENS = 10240
CLIPS = 16
N_SEQ = 16


def draw_vis_index(key, part):
    key = jax.random.fold_in(key, 11)
    owner_count = TOKENS // TOK_DEV

    def one_clip(clip_key):
        key_weights, key_heavy, key_ranks = jax.random.split(clip_key, 3)
        span_ids = jnp.arange(owner_count, dtype=jnp.int32)
        heavy = jax.random.randint(key_heavy, (), 0, owner_count, dtype=jnp.int32)
        weights = jnp.where(span_ids == heavy, 0, jax.random.randint(key_weights, (owner_count,), 4, 8, dtype=jnp.int32))
        running = jnp.cumsum(weights).astype(jnp.int32)
        bounds = (VIS - CAP) * running // running[-1]
        shares = bounds - jnp.concatenate([jnp.zeros((1,), jnp.int32), bounds[:-1]])
        counts = jnp.where(span_ids == heavy, CAP, shares)
        scores = jax.random.randint(key_ranks, (owner_count, TOK_DEV), 0, 2 ** 14, dtype=jnp.int32) * TOK_DEV + jnp.arange(TOK_DEV, dtype=jnp.int32)[None, :]
        ordering = jnp.argsort(scores, axis=1, stable=True)
        ranks = jnp.argsort(ordering, axis=1, stable=True).astype(jnp.int32)
        seen = (ranks < counts[:, None]).reshape(TOKENS)
        places = jnp.arange(TOKENS, dtype=jnp.int32)
        sort_keys = jnp.where(seen, TOKENS - places, -1 - places)
        return lax.top_k(sort_keys, VIS)[1].astype(jnp.int32)
    return jax.vmap(one_clip)(jax.random.split(key, CLIPS))


def draw_w_qkv(key, part):
    key = jax.random.fold_in(key, 7)
    key_normal = jax.random.fold_in(key, 0)
    weights = jax.random.normal(key_normal, (3, D, D), jnp.float32) * D ** (-0.5)
    return weights.astype(jnp.bfloat16)


def spiked(drawn, own_key, source, target, blocks, factor):
    def block_of(position):
        return (jnp.arange(drawn.shape[position]) // (drawn.shape[position] // blocks)).reshape((-1,) + (1,) * (drawn.ndim - 1 - position))

    near = jax.random.permutation(own_key, blocks)[block_of(target)]
    other_side = (block_of(target) + blocks // 2) % blocks
    return jnp.where((block_of(source) == near) | (block_of(source) == other_side), factor * drawn, drawn)


def steps_of(stream_key, extent, cuts, least, largest):
    level, own = 1.0, jax.random.fold_in(stream_key, 6)
    for axis_at, blocks in cuts:
        steps = jnp.exp(jax.random.uniform(jax.random.fold_in(own, axis_at), (blocks,), jnp.float32, least / len(cuts), largest / len(cuts)))
        level = level * jnp.repeat(steps, extent[axis_at] // blocks).reshape([-1 if axis == axis_at else 1 for axis in range(len(extent))])
    return level


def scatter_about(rng, dims, scale, most, shards=(), kind=jnp.bfloat16):
    loudness = steps_of(rng, dims, shards, -0.22, 0.18) if shards else 1.0
    array = jax.random.normal(rng, dims, jnp.float32) * scale * loudness
    return jnp.minimum(jnp.maximum(array, -most), most).astype(kind)


def bell_draw_with(rng, shape, scale, reach, pieces, heavy, kind=jnp.bfloat16):
    values = scale * jax.random.normal(rng, shape, jnp.float32)
    if pieces:
        values = values * steps_of(rng, shape, pieces, -0.22, 0.18)
    return jnp.clip(spiked(values, jax.random.fold_in(rng, 3), *heavy), -reach, reach).astype(kind)


def setup_inputs(seed: int = 0) -> dict:
    streams_of = jax.random.split(jax.random.key(seed), 14)
    patches = scatter_about(streams_of[0], (CLIPS, TOKENS, D), 1.0, 6.0, ((0, 16), (1, 16)))
    vis_index = draw_vis_index(jax.random.fold_in(streams_of[13], 71), 0)
    enc_gain = jnp.clip(1.0 + 0.1 * jax.random.normal(streams_of[2], (D,), jnp.float32), 0.5, 1.5)
    w_qkv = draw_w_qkv(jax.random.fold_in(streams_of[13], 71), 0)
    w_out = scatter_about(streams_of[4], (D, D), 8 ** -0.5, 2.0, ((0, 16),))
    w_embed = scatter_about(streams_of[5], (D, DEC), D ** -0.5, 0.15625, ((1, 256),))
    mask_token = scatter_about(streams_of[6], (DEC,), 1.0, 4.0)
    pos_embed = scatter_about(streams_of[7], (TOKENS, DEC), 0.5, 3.0, ((0, 16),))
    dec_gain = jnp.clip(1.0 + 0.1 * jax.random.normal(streams_of[8], (DEC,), jnp.float32), 0.5, 1.5)
    w_up = scatter_about(streams_of[9], (DEC, HID), DEC ** -0.5, 0.25, ((1, 256),))
    w_down = scatter_about(streams_of[10], (HID, DEC), HID ** -0.5, 0.125, ((0, 256),))
    w_pixel = scatter_about(streams_of[11], (DEC, PIX), DEC ** -0.5, 0.25)
    target = bell_draw_with(streams_of[12], (CLIPS, TOKENS, PIX), 1.0, 6.0, ((0, 16), (1, 16)), (1, 2, 8, 2.0))
    return dict(patches=patches, vis_index=vis_index, enc_gain=enc_gain, w_qkv=w_qkv, w_out=w_out, w_embed=w_embed, mask_token=mask_token, pos_embed=pos_embed, dec_gain=dec_gain, w_up=w_up, w_down=w_down, w_pixel=w_pixel, target=target)


def layer_norm(values, gain):
    values = values.astype(jnp.float32)
    center = lax.optimization_barrier(jnp.mean(values, axis=-1, keepdims=True))
    spread = lax.optimization_barrier(jnp.mean((values - center) ** 2, axis=-1, keepdims=True))
    return (values - center) * lax.rsqrt(spread + 1e-05) * gain.astype(jnp.float32)

def attend_head(triple):
    queries, keys_all, values_all = triple
    scores = jnp.dot(queries, keys_all.T, preferred_element_type=jnp.float32) * HEAD ** (-0.5)
    peak = lax.optimization_barrier(jnp.max(scores, axis=-1, keepdims=True))
    expo = jnp.exp(scores - peak)
    weights_bf = (expo / lax.optimization_barrier(jnp.sum(expo, axis=-1, keepdims=True))).astype(jnp.bfloat16)
    return jnp.dot(weights_bf, values_all, preferred_element_type=jnp.float32).astype(jnp.bfloat16)

def reference(patches, vis_index, enc_gain, w_qkv, w_out, w_embed, mask_token, pos_embed, dec_gain, w_up, w_down, w_pixel, target):
    width_group = D // N_SEQ

    def clip_pass(inputs):
        patch_rows, index_list, target_rows = inputs
        visible = jnp.take(patch_rows, index_list, axis=0)
        normed = layer_norm(visible, enc_gain).astype(jnp.bfloat16)
        parts = [jnp.dot(normed, w_qkv[slot_id], preferred_element_type=jnp.float32).astype(jnp.bfloat16) for slot_id in range(3)]
        split_heads = [part.reshape(VIS, H, HEAD).transpose(1, 0, 2) for part in parts]
        heads_out = lax.map(attend_head, (split_heads[0], split_heads[1], split_heads[2]))
        heads_out = heads_out.transpose(1, 0, 2).reshape(VIS, D)
        out_groups = heads_out.reshape(VIS, N_SEQ, width_group).transpose(1, 0, 2)
        weight_groups = w_out.reshape(N_SEQ, width_group, D)

        def add_group(total, pair):
            group_rows, group_weight = pair
            term = jnp.dot(group_rows, group_weight, preferred_element_type=jnp.float32).astype(jnp.bfloat16)
            term = lax.optimization_barrier(term)
            return (total + term.astype(jnp.float32), None)
        attended, _ = lax.scan(add_group, jnp.zeros((VIS, D), jnp.float32), (out_groups, weight_groups))
        encoded = (visible.astype(jnp.float32) + attended).astype(jnp.bfloat16)
        embedded = jnp.dot(encoded, w_embed, preferred_element_type=jnp.float32).astype(jnp.bfloat16)
        filled = jnp.broadcast_to(mask_token.astype(jnp.float32)[None, :], (TOKENS, DEC))
        filled = filled.at[index_list].set(embedded.astype(jnp.float32))
        dec_input = (filled + pos_embed.astype(jnp.float32)).astype(jnp.bfloat16)
        dec_normed = layer_norm(dec_input, dec_gain).astype(jnp.bfloat16)
        hidden = jax.nn.gelu(jnp.dot(dec_normed, w_up, preferred_element_type=jnp.float32)).astype(jnp.bfloat16)
        decoded = (dec_input.astype(jnp.float32) + jnp.dot(hidden, w_down, preferred_element_type=jnp.float32)).astype(jnp.bfloat16)
        predicted = jnp.dot(decoded, w_pixel, preferred_element_type=jnp.float32)
        seen_flag = jnp.zeros((TOKENS,), jnp.float32).at[index_list].set(1.0)
        resid = ((predicted - target_rows.astype(jnp.float32)) * (1.0 - seen_flag)[:, None]).astype(jnp.bfloat16)
        pixel_term = jnp.dot(decoded.T, resid, preferred_element_type=jnp.float32) * (2.0 / PIX)
        return (decoded, pixel_term)
    decoded_all, terms = lax.map(clip_pass, (patches, vis_index, target))
    return (decoded_all, terms)
```

```python
import jax
import jax.numpy as jnp
from jax import lax
from jax.experimental import pallas as pl
from jax.experimental.pallas import tpu as pltpu
from jax.sharding import PartitionSpec as P

D = 1408
HEAD = 88
HPAD = 96
DEC = 512
HID = 2048
PIX = 1176
TOK = 640
CAP = 128
VIS = 1024
N = 16
ROWS = VIS // N
HALF = 768
F32 = jnp.float32
BF16 = jnp.bfloat16
MESH = pl.DeviceIdType.MESH
EXP_SCALE = HEAD ** (-0.5) * 1.4426950408889634

NT = (((1,), (1,)), ((), ()))
NN = (((1,), (0,)), ((), ()))
TN = (((0,), (0,)), ((), ()))
TT = (((0,), (1,)), ((), ()))


def dot(left, right, dims):
    return lax.dot_general(left, right, dims, preferred_element_type=F32)


def iota(shape, axis):
    return lax.broadcasted_iota(jnp.int32, shape, axis)


def norm_rows(values, gain):
    center = jnp.mean(values, axis=-1, keepdims=True)
    spread = jnp.mean((values - center) ** 2, axis=-1, keepdims=True)
    return ((values - center) * lax.rsqrt(spread + 1e-05) * gain).astype(BF16)


def rcopy(src, dst, send_sem, recv_sem, dev):
    return pltpu.make_async_remote_copy(
        src_ref=src,
        dst_ref=dst,
        send_sem=send_sem,
        recv_sem=recv_sem,
        device_id=dev,
        device_id_type=MESH,
    )


class PlaneGather:
    def __init__(self, buf, send, recv, clip, seq, cuts):
        self.buf, self.send, self.recv, self.clip = buf, send, recv, clip
        self.x, self.y = seq // 4, seq % 4
        self.cuts = cuts
        self.used = [0, 0]
        self.started = []

    def rank(self, fam, p, q):
        dx, dy = (p, q) if fam == 0 else (q, p)
        return ((self.x + dx + 4) % 4) * 4 + (self.y + dy + 4) % 4

    def piece(self, fam, p, q, part):
        lo, mid, hi = self.cuts[fam]
        lo, hi = ((lo, hi), (lo, mid), (mid, hi))[part]
        return self.buf.at[self.rank(fam, p, q), pl.ds(lo, hi - lo)]

    def copy(self, fam, p, q, part, to, slot):
        ref = self.piece(fam, p, q, part)
        rank = self.rank(fam, p, q)
        return rcopy(
            ref,
            ref,
            self.send.at[fam, slot],
            self.recv.at[fam, rank, 1 if part == 2 else 0],
            (self.clip, self.rank(fam, *to)),
        )

    def go(self, fam, p, q, part, to):
        made = self.copy(fam, p, q, part, to, self.used[fam])
        self.used[fam] += 1
        made.start()
        self.started.append(made)

    def got(self, fam, p, q, part):
        self.copy(fam, p, q, part, (1, 0), 0).wait_recv()

    def spread(self, fam, p):
        self.go(fam, p, 0, 0, (0, 1))
        self.go(fam, p, 0, 0, (0, -1))

    def first(self):
        for fam in (0, 1):
            self.go(fam, 0, 0, 0, (1, 0))
            self.go(fam, 0, 0, 0, (-1, 0))
        for fam in (0, 1):
            self.spread(fam, 0)

    def second(self):
        for fam in (0, 1):
            self.got(fam, -1, 0, 0)
            self.go(fam, -1, 0, 1, (1, 0))
            self.got(fam, 1, 0, 0)
            self.go(fam, 1, 0, 2, (-1, 0))
        for fam in (0, 1):
            self.spread(fam, -1)
            self.spread(fam, 1)

    def third(self):
        for fam in (0, 1):
            self.got(fam, 2, 0, 1)
            self.got(fam, 2, 0, 2)
            self.spread(fam, 2)

    def relay(self, p):
        for fam in (0, 1):
            self.got(fam, p, -1, 0)
            self.go(fam, p, -1, 1, (0, 1))
            self.got(fam, p, 1, 0)
            self.go(fam, p, 1, 2, (0, -1))

    def last(self, p):
        for fam in (0, 1):
            self.got(fam, p, 2, 1)
            self.got(fam, p, 2, 2)

    def finish(self):
        for made in self.started:
            made.wait_send()


class LineGather:
    def __init__(self, buf, send, recv, side_send, side_recv, clip, seq):
        self.buf, self.send, self.recv = buf, send, recv
        self.side_send, self.side_recv = side_send, side_recv
        self.clip, self.seq = clip, seq
        self.other = clip + 1 - 2 * (clip % 2)
        self.half = buf.shape[1] // 2
        self.started = []

    def block(self, step):
        return (self.clip + 2 * step + 16) % 16

    def piece(self, step, part):
        rows = ((0, 2 * self.half), (0, self.half), (self.half, self.half))[part]
        return self.buf.at[self.block(step), pl.ds(*rows)]

    def copy(self, step, part, way, slot):
        ref = self.piece(step, part)
        return rcopy(
            ref,
            ref,
            self.send.at[slot],
            self.recv.at[self.block(step), 1 if part == 2 else 0],
            (self.block(way), self.seq),
        )

    def go(self, step, part, way, slot):
        made = self.copy(step, part, way, slot)
        made.start()
        self.started.append(made)

    def side(self, step):
        ref = self.buf.at[self.block(step)]
        slot = step + 3
        made = rcopy(
            ref,
            ref,
            self.side_send.at[slot],
            self.side_recv.at[self.block(step)],
            (self.other, self.seq),
        )
        made.start()
        self.started.append(made)

    def step(self, t):
        if t == 0:
            self.go(0, 0, 1, 0)
            self.go(0, 0, -1, 1)
            self.side(0)
            return
        if t == 4:
            self.copy(4, 1, 1, 0).wait_recv()
            self.copy(4, 2, 1, 0).wait_recv()
            self.side(4)
            return
        up, down = (1, 2) if t == 3 else (0, 0)
        self.copy(-t, 0, 1, 0).wait_recv()
        self.go(-t, up, 1, 2 * t)
        self.copy(t, 0, 1, 0).wait_recv()
        self.go(t, down, -1, 2 * t + 1)
        self.side(-t)
        self.side(t)

    def sides(self):
        for step in range(-3, 5):
            block = (self.other + 2 * step + 16) % 16
            ref = self.buf.at[block]
            rcopy(
                ref, ref, self.side_send.at[0], self.side_recv.at[block], (self.other, self.seq)
            ).wait_recv()

    def finish(self):
        for made in self.started:
            made.wait_send()


def kernel(
    patches,
    vis64,
    enc_gain,
    w_qkv,
    w_out,
    w_embed,
    mask_token,
    pos_embed,
    dec_gain,
    w_up,
    w_down,
    w_pixel,
    target,
    decoded_out,
    grad_out,
    patch_v,
    pos_v,
    pix_v,
    tgt_v,
    ud_mine,
    e_mine,
    pick_v,
    seen_v,
    visible_v,
    row_send,
    row_recv,
    rows_v,
    code_v,
    qv_v,
    keys_v,
    ho_v,
    ho_send,
    ho_recv,
    wo_v,
    ud_v,
    e_v,
    up_v,
    down_v,
    emb_v,
    acc_v,
    dec_v,
    dn_v,
    resid_v,
    g_send,
    g_recv,
    load_sem,
    l1_s,
    l1_r,
    a2a_s,
    a2a_r,
    ag_s,
    ag_r,
    wo_s,
    wo_r,
    wside_s,
    wside_r,
    zu_s,
    zu_r,
    zus_s,
    zus_r,
    ze_s,
    ze_r,
    zes_s,
    zes_r,
    ho_s,
    ho_r,
    g_s,
    g_r,
):
    clip, seq = lax.axis_index("clip"), lax.axis_index("seq")
    core = clip % 2
    other = clip + 1 - 2 * core

    loads = [
        pltpu.make_async_copy(src, dst, load_sem.at[i])
        for i, (src, dst) in enumerate(
            ((patches, patch_v), (pos_embed, pos_v), (w_pixel, pix_v), (target, tgt_v))
        )
    ]
    for load in loads:
        load.start()

    barrier = pltpu.get_barrier_semaphore()

    @pl.loop(1, N)
    def _(o):
        pl.semaphore_signal(
            barrier, inc=1, device_id=(clip, (seq + o) % N), device_id_type=MESH
        )

    for dev in (other, (clip + 2) % 16, (clip + 14) % 16):
        pl.semaphore_signal(barrier, inc=1, device_id=(dev, seq), device_id_type=MESH)

    ud_mine[...] = jnp.concatenate(
        [w_up[...].astype(F32), w_down[...].astype(F32)], axis=0
    ).astype(BF16)
    emb_rows = jnp.concatenate([w_embed[...].astype(F32), jnp.zeros((2, 128), F32)], axis=1)
    packed = jnp.zeros((16, 256), F32)
    row16 = iota((16, 256), 0)
    for a in range(2):
        for q in range(6):
            line = jnp.broadcast_to(emb_rows[a : a + 1, q * 256 : (q + 1) * 256], (16, 256))
            packed = jnp.where(row16 == a * 8 + q, line, packed)
    e_mine[...] = packed.astype(BF16)
    my16 = pl.ds(pl.multiple_of(seq * 16, 16), 16)
    ud_v[clip, my16, :] = ud_mine[...]
    e_v[clip, my16, :] = e_mine[...]

    pl.semaphore_wait(barrier, N - 1 + 3)

    def l1_copies(peer, slot, src):
        at = pl.ds(pl.multiple_of(src * 16, 16), 16)
        dev = (clip, peer)
        return (
            rcopy(ud_mine, ud_v.at[clip, at], l1_s.at[0, slot], l1_r.at[0, src], dev),
            rcopy(e_mine, e_v.at[clip, at], l1_s.at[1, slot], l1_r.at[1, src], dev),
        )

    @pl.loop(1, N)
    def _(o):
        for made in l1_copies((seq + o) % N, o, seq):
            made.start()

    v64 = vis64[...]
    own64 = jnp.zeros((ROWS, N), jnp.int32)
    for d in range(1, N):
        own64 = own64 + (v64 >= d * TOK).astype(jnp.int32)
    mine = jnp.where(own64 == seq, v64 - seq * TOK + 1, 0)
    place = mine[0:8]
    for a in range(1, 8):
        place = place + mine[8 * a : 8 * a + 8]
    spot = jnp.concatenate([place[:, j : j + 1] for j in range(N)], axis=0) - 1
    pick = (iota((CAP, TOK), 1) == spot).astype(F32)
    seen_v[...] = jnp.sum(pick, axis=0, keepdims=True)
    pick_v[...] = pick.astype(BF16)
    loads[0].wait()
    visible = dot(pick_v[...], patch_v[...], NN)
    visible_v[...] = visible
    center = jnp.mean(visible, axis=-1, keepdims=True)
    spread = jnp.mean((visible - center) ** 2, axis=-1, keepdims=True)
    normed = (visible - center) * lax.rsqrt(spread + 1e-05) * enc_gain[...]
    for j in range(N):
        row_send[j] = normed[8 * j : 8 * j + 8].astype(BF16)

    def a2a_copy(peer, slot, src):
        return rcopy(
            row_send.at[peer], row_recv.at[src], a2a_s.at[slot], a2a_r.at[src], (clip, peer)
        )

    row_recv[seq] = row_send[seq]

    @pl.loop(1, N)
    def _(o):
        a2a_copy((seq + o) % N, o, seq).start()

    @pl.loop(1, N)
    def _(o):
        for made in l1_copies(seq, 0, (seq + o) % N):
            made.wait_recv()

    line_ud = LineGather(ud_v, zu_s, zu_r, zus_s, zus_r, clip, seq)
    line_e = LineGather(e_v, ze_s, ze_r, zes_s, zes_r, clip, seq)
    line_ud.step(0)

    wide = jnp.concatenate([w_out[...].astype(F32), jnp.zeros((HPAD - HEAD, D), F32)], axis=0)
    wo_v[0, seq] = wide[:, :HALF].astype(BF16)
    wo_v[1, seq] = jnp.concatenate(
        [wide[:, HALF:], jnp.zeros((HPAD, 2 * HALF - D), F32)], axis=1
    ).astype(BF16)

    low = iota((ROWS, 1), 0) % 8
    for j in range(N):
        code = own64[:, j : j + 1] * CAP + j * 8 + low
        code_v[j * ROWS : (j + 1) * ROWS, :] = (
            (iota((ROWS, N * CAP), 1) == code).astype(F32).astype(BF16)
        )

    own_me = jnp.sum(
        jnp.where(iota((ROWS, N), 1) == seq, own64, 0), axis=1, keepdims=True
    )
    lane = iota((ROWS, N * 8), 1)
    gather = ((own_me == lane // 8) & (low == lane % 8)).astype(F32).astype(BF16)

    @pl.loop(1, N)
    def _(o):
        a2a_copy(seq, 0, (seq + o) % N).wait_recv()

    arrived = jnp.concatenate([row_recv[d].astype(F32) for d in range(N)], axis=0).astype(BF16)
    rows_v[seq] = dot(gather, arrived, NN).astype(BF16)

    rows_ag = PlaneGather(rows_v, ag_s, ag_r, clip, seq, ((0, 16, 32), (32, 48, 64)))
    rows_ag.first()
    rows_ag.second()
    rows_ag.third()
    wo_ag = PlaneGather(wo_v.at[core], wo_s, wo_r, clip, seq, ((0, 32, 48), (48, 80, 96)))
    wo_ag.first()
    line_ud.step(1)
    for p in (0, -1, 1, 2):
        rows_ag.relay(p)
    wo_ag.second()
    for p in (0, -1, 1, 2):
        rows_ag.last(p)
    wo_ag.third()

    zeros_q = jnp.zeros((HPAD - HEAD, 256), F32)

    @pl.loop(0, 4)
    def _(b):
        rows = rows_v[pl.ds(b * 4, 4)].reshape(256, D)
        at = pl.ds(pl.multiple_of(b * 256, 256), 256)
        for i, top in ((0, 0), (2, HPAD)):
            part = dot(w_qkv[i], rows, NT)
            qv_v[pl.ds(top, HPAD), at] = jnp.concatenate([part, zeros_q], axis=0).astype(BF16)
        keys = dot(rows, w_qkv[1], NT)
        keys_v[at, :] = jnp.concatenate(
            [keys, jnp.zeros((256, HPAD - HEAD), F32)], axis=1
        ).astype(BF16)

    line_ud.step(2)
    wo_ag.relay(0)
    wo_ag.relay(-1)

    @pl.loop(0, 4)
    def _(b):
        at = pl.ds(pl.multiple_of(b * 256, 256), 256)
        scores = dot(keys_v[...], qv_v[pl.ds(0, HPAD), at], NN)
        peak = jnp.max(scores, axis=0, keepdims=True)
        expo = jnp.exp2((scores - peak) * EXP_SCALE)
        total = jnp.sum(expo, axis=0, keepdims=True)
        probs = (expo * (1.0 / total)).astype(BF16)
        ho_v[:, at] = dot(qv_v[pl.ds(HPAD, HPAD), :], probs, NN).astype(BF16)

    wo_ag.relay(1)
    wo_ag.relay(2)
    line_ud.step(3)
    line_e.step(0)

    @pl.loop(0, N // 2)
    def _(h):
        two = dot(
            ho_v[...], code_v[:, pl.ds(pl.multiple_of(h * 256, 256), 256)], NN
        ).astype(BF16)
        ho_send[2 * h] = two[:, :CAP]
        ho_send[2 * h + 1] = two[:, CAP:]

    def ho_copy(peer, slot, src):
        return rcopy(
            ho_send.at[peer], ho_recv.at[src], ho_s.at[slot], ho_r.at[src], (clip, peer)
        )

    ho_recv[seq] = ho_send[seq]

    @pl.loop(1, N)
    def _(o):
        ho_copy((seq + o) % N, o, seq).start()

    for p in (0, -1, 1, 2):
        wo_ag.last(p)

    def wo_side(half, j):
        ref = wo_v.at[half, j]
        return rcopy(ref, ref, wside_s.at[j], wside_r.at[j], (other, seq))

    @pl.loop(1, N)
    def _(o):
        wo_side(core, (seq + o) % N).start()

    line_ud.step(4)
    line_e.step(1)
    line_ud.sides()

    r256, c256 = iota((256, 256), 0), iota((256, 256), 1)
    unit = r256 % 128
    order_ud = (c256 == (unit // 8) * 16 + unit % 8 + 8 * (r256 // 128)).astype(F32).astype(BF16)

    @pl.loop(0, N)
    def _(b):
        both = dot(order_ud, ud_v[b], NN).astype(BF16)
        at = pl.ds(pl.multiple_of(b * 128, 128), 128)
        up_v[at, :] = both[:128]
        down_v[at, :] = both[128:]

    def mlp(dec_in, count):
        dn_v[0:count, :] = norm_rows(dec_in.astype(F32), dec_gain[...])
        acc_v[0:count, :] = dec_in.astype(F32)

        @pl.loop(0, 4)
        def _(h):
            at = pl.ds(pl.multiple_of(h * 512, 512), 512)
            hidden = jax.nn.gelu(dot(dn_v[0:count, :], up_v[at, :], NT)).astype(BF16)
            acc_v[0:count, :] += dot(hidden, down_v[at, :], NN)

        return acc_v[0:count, :].astype(BF16)

    loads[1].wait()
    dec_in = (mask_token[...].astype(F32) + pos_v[...].astype(F32)).astype(BF16)
    dec_v[...] = mlp(dec_in, TOK)
    line_e.step(2)
    loads[2].wait()
    loads[3].wait()
    keep = 1.0 - seen_v[...]
    for lo, hi in ((0, 512), (512, 1024), (1024, PIX)):
        predicted = dot(pix_v[lo:hi, :], dec_v[...], NT)
        resid_v[lo:hi, :] = ((predicted - tgt_v[lo:hi, :].astype(F32)) * keep).astype(BF16)
    line_e.step(3)

    def g_copy(peer, slot, src):
        return rcopy(g_send.at[peer], g_recv.at[src], g_s.at[slot], g_r.at[src], (clip, peer))

    for quarter in range(4):
        term = dot(dec_v[:, quarter * 128 : (quarter + 1) * 128], resid_v[...], TT) * (2.0 / PIX)
        for i in range(4):
            g_send[quarter * 4 + i] = term[32 * i : 32 * i + 32].astype(BF16)

    @pl.loop(1, N)
    def _(o):
        g_copy((seq + o) % N, o, seq).start()

    line_e.step(4)
    line_e.sides()
    r192, c192 = iota((192, 256), 0), iota((192, 256), 1)
    order_e = (c192 == (r192 % 32) * 8 + r192 // 32).astype(F32).astype(BF16)

    @pl.loop(0, N)
    def _(b):
        lines = dot(order_e, e_v[b], NN).astype(BF16)
        at = pl.ds(pl.multiple_of(b * 32, 32), 32)
        for q in range(6):
            emb_v[at, q * 256 : (q + 1) * 256] = lines[q * 32 : (q + 1) * 32]

    @pl.loop(1, N)
    def _(o):
        ho_copy(seq, 0, (seq + o) % N).wait_recv()

    @pl.loop(1, N)
    def _(o):
        wo_side(1 - core, (seq + o) % N).wait_recv()

    heads = ho_recv[...].reshape(N * HPAD, CAP)
    attended = jnp.concatenate(
        [dot(heads, wo_v[half].reshape(N * HPAD, HALF), TN) for half in range(2)], axis=1
    )
    encoded = (visible_v[...] + attended[:, :D]).astype(BF16)
    embedded = dot(encoded, emb_v[:, :D], NT).astype(BF16)
    pos_rows = dot(pick_v[...], pos_v[...], NN)
    dec_in = (embedded.astype(F32) + pos_rows).astype(BF16)
    vis_dec = mlp(dec_in, CAP)
    pick_dot = dot(pick_v[...], vis_dec, TN)
    seen_col = dot(pick_v[...], jnp.ones((CAP, DEC), BF16), TN)
    decoded_out[...] = jnp.where(seen_col > 0.5, pick_dot, dec_v[...].astype(F32)).astype(BF16)

    total = g_send[seq].astype(F32)
    for o in range(1, N):
        src = (seq + o) % N
        g_copy(seq, 0, src).wait_recv()
        total = total + g_recv[src].astype(F32)
    grad_out[...] = total

    @pl.loop(1, N)
    def _(o):
        peer = (seq + o) % N
        for made in l1_copies(peer, o, seq):
            made.wait_send()
        a2a_copy(peer, o, seq).wait_send()
        ho_copy(peer, o, seq).wait_send()
        g_copy(peer, o, seq).wait_send()
        wo_side(core, peer).wait_send()

    rows_ag.finish()
    wo_ag.finish()
    line_ud.finish()
    line_e.finish()


def shards(
    patches,
    vis_index,
    enc_gain,
    w_qkv,
    w_out,
    w_embed,
    mask_token,
    pos_embed,
    dec_gain,
    w_up,
    w_down,
    w_pixel,
    target,
):
    vmem = pl.BlockSpec(memory_space=pltpu.VMEM)
    hbm = pl.BlockSpec(memory_space=pl.ANY)
    dma = pltpu.SemaphoreType.DMA
    decoded, grad = pl.pallas_call(
        kernel,
        out_shape=(
            jax.ShapeDtypeStruct((TOK, DEC), BF16),
            jax.ShapeDtypeStruct((DEC // N, PIX), F32),
        ),
        in_specs=[hbm, vmem, vmem, vmem, vmem, vmem, vmem, hbm, vmem, vmem, vmem, hbm, hbm],
        out_specs=(vmem, vmem),
        scratch_shapes=[
            pltpu.VMEM((TOK, D), BF16),
            pltpu.VMEM((TOK, DEC), BF16),
            pltpu.VMEM((PIX, DEC), BF16),
            pltpu.VMEM((PIX, TOK), BF16),
            pltpu.VMEM((16, 512), BF16),
            pltpu.VMEM((16, 256), BF16),
            pltpu.VMEM((CAP, TOK), BF16),
            pltpu.VMEM((1, TOK), F32),
            pltpu.VMEM((CAP, D), F32),
            pltpu.VMEM((N, 8, D), BF16),
            pltpu.VMEM((N, 8, D), BF16),
            pltpu.VMEM((N, ROWS, D), BF16),
            pltpu.VMEM((VIS, N * CAP), BF16),
            pltpu.VMEM((2 * HPAD, VIS), BF16),
            pltpu.VMEM((VIS, HPAD), BF16),
            pltpu.VMEM((HPAD, VIS), BF16),
            pltpu.VMEM((N, HPAD, CAP), BF16),
            pltpu.VMEM((N, HPAD, CAP), BF16),
            pltpu.VMEM((2, N, HPAD, HALF), BF16),
            pltpu.VMEM((N, 256, 512), BF16),
            pltpu.VMEM((N, 256, 256), BF16),
            pltpu.VMEM((HID, DEC), BF16),
            pltpu.VMEM((HID, DEC), BF16),
            pltpu.VMEM((DEC, 2 * HALF), BF16),
            pltpu.VMEM((TOK, DEC), F32),
            pltpu.VMEM((TOK, DEC), BF16),
            pltpu.VMEM((TOK, DEC), BF16),
            pltpu.VMEM((PIX, TOK), BF16),
            pltpu.VMEM((N, DEC // N, PIX), BF16),
            pltpu.VMEM((N, DEC // N, PIX), BF16),
            dma((4,)),
            dma((2, N)),
            dma((2, N)),
            dma((N,)),
            dma((N,)),
            dma((2, 20)),
            dma((2, N, 2)),
            dma((2, 20)),
            dma((2, N, 2)),
            dma((N,)),
            dma((N,)),
            dma((8,)),
            dma((N, 2)),
            dma((8,)),
            dma((N,)),
            dma((8,)),
            dma((N, 2)),
            dma((8,)),
            dma((N,)),
            dma((N,)),
            dma((N,)),
            dma((N,)),
            dma((N,)),
        ],
        compiler_params=pltpu.CompilerParams(
            collective_id=0, has_side_effects=True, vmem_limit_bytes=60 * 1024 * 1024
        ),
    )(
        patches[0],
        vis_index.reshape(ROWS, N),
        enc_gain.reshape(1, D),
        jnp.transpose(w_qkv, (0, 2, 1)),
        w_out,
        w_embed.T,
        mask_token.reshape(1, DEC),
        pos_embed,
        dec_gain.reshape(1, DEC),
        w_up.T,
        w_down,
        w_pixel.T,
        target[0].T,
    )
    return decoded[None], grad[None]


def solution(mesh):
    placed = (
        P("clip", "seq", None),
        P("clip", None),
        P(),
        P(None, None, "seq"),
        P("seq", None),
        P(None, ("clip", "seq")),
        P(),
        P("seq", None),
        P(),
        P(None, ("clip", "seq")),
        P(("clip", "seq"), None),
        P(),
        P("clip", "seq", None),
    )
    return jax.shard_map(
        shards,
        mesh=mesh,
        in_specs=placed,
        out_specs=(P("clip", "seq", None), P("clip", "seq", None)),
        check_vma=False,
    )
```

```python
import jax
import jax.numpy as jnp
from jax import lax
from jax.experimental import pallas as pl
from jax.experimental.pallas import tpu as pltpu
from jax.sharding import PartitionSpec as P

D = 1408
HEAD = 88
HPAD = 96
DEC = 512
HID = 2048
PIX = 1176
TOK = 640
CAP = 128
VIS = 1024
N = 16
ROWS = VIS // N
HALF = 768
F32 = jnp.float32
BF16 = jnp.bfloat16
MESH = pl.DeviceIdType.MESH
EXP_SCALE = HEAD ** (-0.5) * 1.4426950408889634

NT = (((1,), (1,)), ((), ()))
NN = (((1,), (0,)), ((), ()))
TN = (((0,), (0,)), ((), ()))
TT = (((0,), (1,)), ((), ()))


def dot(left, right, dims):
    return lax.dot_general(left, right, dims, preferred_element_type=F32)


def iota(shape, axis):
    return lax.broadcasted_iota(jnp.int32, shape, axis)


def norm_rows(values, gain):
    center = jnp.mean(values, axis=-1, keepdims=True)
    spread = jnp.mean((values - center) ** 2, axis=-1, keepdims=True)
    return ((values - center) * lax.rsqrt(spread + 1e-05) * gain).astype(BF16)


def rcopy(src, dst, send_sem, recv_sem, dev):
    return pltpu.make_async_remote_copy(
        src_ref=src,
        dst_ref=dst,
        send_sem=send_sem,
        recv_sem=recv_sem,
        device_id=dev,
        device_id_type=MESH,
    )


class PlaneGather:
    def __init__(self, buf, send, recv, clip, seq, cuts):
        self.buf, self.send, self.recv, self.clip = buf, send, recv, clip
        self.x, self.y = seq // 4, seq % 4
        self.cuts = cuts

    def rank(self, fam, p, q):
        dx, dy = (p, q) if fam == 0 else (q, p)
        return ((self.x + dx + 4) % 4) * 4 + (self.y + dy + 4) % 4

    def piece(self, fam, p, q, part):
        lo, mid, hi = self.cuts[fam]
        lo, hi = ((lo, hi), (lo, mid), (mid, hi))[part]
        return self.buf.at[self.rank(fam, p, q), pl.ds(lo, hi - lo)]

    def go(self, fam, p, q, part, to, stage):
        ref = self.piece(fam, p, q, part)
        dev = (self.clip, self.rank(fam, *to))
        rcopy(ref, ref, self.send, self.recv.at[stage], dev).start()

    def got(self, stage, pieces):
        ref = self.buf.at[pl.ds(0, pieces)]
        rcopy(ref, ref, self.send, self.recv.at[stage], (self.clip, self.rank(0, 1, 0))).wait_recv()

    def spread(self, fam, p):
        self.go(fam, p, 0, 0, (0, 1), 2 + p % 4)
        self.go(fam, p, 0, 0, (0, -1), 2 + p % 4)

    def first(self):
        for fam in (0, 1):
            self.go(fam, 0, 0, 0, (1, 0), 0)
            self.go(fam, 0, 0, 0, (-1, 0), 0)
        for fam in (0, 1):
            self.spread(fam, 0)

    def second(self):
        self.got(0, 2)
        for fam in (0, 1):
            self.go(fam, -1, 0, 1, (1, 0), 1)
            self.go(fam, 1, 0, 2, (-1, 0), 1)
        for fam in (0, 1):
            self.spread(fam, -1)
            self.spread(fam, 1)

    def third(self):
        self.got(1, 1)
        for fam in (0, 1):
            self.spread(fam, 2)

    def relay(self, p):
        self.got(2 + p % 4, 2)
        for fam in (0, 1):
            self.go(fam, p, -1, 1, (0, 1), 6 + p % 4)
            self.go(fam, p, 1, 2, (0, -1), 6 + p % 4)

    def last(self, p):
        self.got(6 + p % 4, 1)

    def finish(self):
        ref = self.buf.at[pl.ds(0, N - 1)]
        rcopy(ref, ref, self.send, self.recv.at[0], (self.clip, self.rank(0, 1, 0))).wait_send()


class LineGather:
    def __init__(self, buf, send, recv, side_send, side_recv, clip, seq, subs):
        self.buf, self.send, self.recv = buf, send, recv
        self.side_send, self.side_recv = side_send, side_recv
        self.clip, self.seq, self.subs = clip, seq, subs
        self.other = clip + 1 - 2 * (clip % 2)
        self.rows = buf.shape[1]

    def block(self, step):
        return (self.clip + 2 * step + 16) % 16

    def go(self, step, lo, size, way, sem):
        ref = self.buf.at[self.block(step), pl.ds(lo, size)]
        rcopy(ref, ref, self.send, self.recv.at[sem], (self.block(way), self.seq)).start()

    def got(self, sem, rows):
        ref = self.buf.at[0, pl.ds(0, rows)]
        rcopy(ref, ref, self.send, self.recv.at[sem], (self.block(1), self.seq)).wait_recv()

    def side(self, step):
        ref = self.buf.at[self.block(step)]
        rcopy(ref, ref, self.side_send, self.side_recv, (self.other, self.seq)).start()

    def step(self, t, sub=0):
        size = self.rows // self.subs
        sem = t * self.subs + sub
        half = self.rows // 2
        done = sub == self.subs - 1
        if t == 0:
            self.go(0, sub * size, size, 1, sem)
            self.go(0, sub * size, size, -1, sem)
            if done:
                self.side(0)
        elif t == 4:
            self.got(sem - self.subs, half if self.subs == 2 else self.rows)
            if done:
                self.side(4)
        else:
            both = self.buf.at[pl.ds(0, 2), pl.ds(0, size)]
            rcopy(
                both, both, self.send, self.recv.at[sem - self.subs], (self.block(1), self.seq)
            ).wait_recv()
            if t < 3:
                self.go(-t, sub * size, size, 1, sem)
                self.go(t, sub * size, size, -1, sem)
            else:
                if sub == 0:
                    self.go(-3, 0, half, 1, sem)
                if done:
                    self.go(3, half, half, -1, sem)
            if done:
                self.side(-t)
                self.side(t)

    def sides(self):
        ref = self.buf.at[pl.ds(0, 8)]
        rcopy(ref, ref, self.side_send, self.side_recv, (self.other, self.seq)).wait_recv()

    def finish(self):
        ref = self.buf.at[pl.ds(0, 7)]
        rcopy(ref, ref, self.send, self.recv.at[0], (self.block(1), self.seq)).wait_send()
        ref = self.buf.at[pl.ds(0, 8)]
        rcopy(ref, ref, self.side_send, self.side_recv, (self.other, self.seq)).wait_send()


def kernel(
    patches,
    vis,
    enc_gain,
    w_qkv,
    w_out,
    w_embed,
    mask_token,
    pos_embed,
    dec_gain,
    w_up,
    w_down,
    w_pixel,
    target,
    decoded_out,
    grad_out,
    patch_v,
    pos_v,
    pix_v,
    tgt_v,
    ud_mine,
    e_mine,
    pick_v,
    seen_v,
    visible_v,
    row_send,
    row_recv,
    rows_v,
    code_v,
    qv_v,
    keys_v,
    ho_v,
    ho_send,
    ho_recv,
    wo_v,
    ud_v,
    e_v,
    up_v,
    down_v,
    emb_v,
    acc_v,
    dec_v,
    dn_v,
    g_send,
    g_recv,
    g_mid,
    g_last,
    load_sem,
    ud_s,
    e_s,
    a2a_s,
    ho_s,
    g_s,
    wside_s,
    ag_s,
    ag_r,
    wo_s,
    wo_r,
    zu_s,
    zu_r,
    ze_s,
    ze_r,
):
    clip, seq = lax.axis_index("clip"), lax.axis_index("seq")
    core = clip % 2
    other = clip + 1 - 2 * core

    loads = [
        pltpu.make_async_copy(src, dst, load_sem.at[i])
        for i, (src, dst) in enumerate(
            ((patches, patch_v), (pos_embed, pos_v), (w_pixel, pix_v), (target, tgt_v))
        )
    ]
    for load in loads:
        load.start()

    barrier = pltpu.get_barrier_semaphore()

    @pl.loop(1, N)
    def _(o):
        pl.semaphore_signal(
            barrier, inc=1, device_id=(clip, (seq + o) % N), device_id_type=MESH
        )

    for dev in (other, (clip + 2) % 16, (clip + 14) % 16):
        pl.semaphore_signal(barrier, inc=1, device_id=(dev, seq), device_id_type=MESH)

    ud_mine[...] = jnp.concatenate(
        [w_up[...].astype(F32), w_down[...].astype(F32)], axis=0
    ).astype(BF16)
    emb_rows = jnp.concatenate([w_embed[...].astype(F32), jnp.zeros((2, 128), F32)], axis=1)
    packed = jnp.zeros((16, 256), F32)
    row16 = iota((16, 256), 0)
    for a in range(2):
        for q in range(6):
            line = jnp.broadcast_to(emb_rows[a : a + 1, q * 256 : (q + 1) * 256], (16, 256))
            packed = jnp.where(row16 == a * 8 + q, line, packed)
    e_mine[...] = packed.astype(BF16)
    my16 = pl.ds(pl.multiple_of(seq * 16, 16), 16)
    ud_v[clip, my16, :] = ud_mine[...]
    e_v[clip, my16, :] = e_mine[...]

    def all_peers(copy):
        @pl.loop(1, N)
        def _(o):
            copy((seq + o) % N).start()

    next_dev = (clip, (seq + 1) % N)

    def both(src, dst, sems):
        return rcopy(src, dst, sems.at[0], sems.at[1], next_dev)

    def ud_copy(peer):
        return rcopy(ud_mine, ud_v.at[clip, my16], ud_s.at[0], ud_s.at[1], (clip, peer))

    def e_copy(peer):
        return rcopy(e_mine, e_v.at[clip, my16], e_s.at[0], e_s.at[1], (clip, peer))

    def a2a_copy(peer):
        return rcopy(row_send.at[peer], row_recv.at[seq], a2a_s.at[0], a2a_s.at[1], (clip, peer))

    def ho_copy(peer):
        return rcopy(ho_send.at[peer], ho_recv.at[seq], ho_s.at[0], ho_s.at[1], (clip, peer))

    many = pl.ds(0, N - 1)
    ud_all = ud_v.at[clip, pl.ds(0, 16 * (N - 1))]
    e_all = e_v.at[clip, pl.ds(0, 16 * (N - 1))]
    ud_wait = both(ud_all, ud_all, ud_s)
    e_wait = both(e_all, e_all, e_s)
    a2a_wait = both(row_send.at[many], row_recv.at[many], a2a_s)
    ho_wait = both(ho_send.at[many], ho_recv.at[many], ho_s)

    token = vis[...]
    here = iota((ROWS, VIS), 1) // N == iota((ROWS, VIS), 0)
    column = (iota((VIS, N), 0) % N == iota((VIS, N), 1)).astype(F32).astype(BF16)

    def digit(values):
        spread = jnp.where(here, jnp.broadcast_to(values, (ROWS, VIS)), 0)
        return dot(spread.astype(F32).astype(BF16), column, NN)

    v64 = (digit(token // 128) * 128.0 + digit(token % 128)).astype(jnp.int32)
    own64 = jnp.zeros((ROWS, N), jnp.int32)
    for d in range(1, N):
        own64 = own64 + (v64 >= d * TOK).astype(jnp.int32)
    mine = jnp.where(own64 == seq, v64 - seq * TOK + 1, 0)
    place = mine[0:8]
    for a in range(1, 8):
        place = place + mine[8 * a : 8 * a + 8]
    spot = jnp.concatenate([place[:, j : j + 1] for j in range(N)], axis=0) - 1
    pick = (iota((CAP, TOK), 1) == spot).astype(F32)
    seen_v[...] = jnp.sum(pick, axis=0, keepdims=True)
    pick_v[...] = pick.astype(BF16)
    loads[0].wait()
    visible = dot(pick_v[...], patch_v[...], NN)
    visible_v[...] = visible
    center = jnp.mean(visible, axis=-1, keepdims=True)
    spread = jnp.mean((visible - center) ** 2, axis=-1, keepdims=True)
    normed = (visible - center) * lax.rsqrt(spread + 1e-05) * enc_gain[...].reshape(1, D)
    for j in range(N):
        row_send[j] = normed[8 * j : 8 * j + 8].astype(BF16)
    row_recv[seq] = row_send[seq]

    pl.semaphore_wait(barrier, N - 1 + 3)
    all_peers(ud_copy)
    all_peers(a2a_copy)

    line_ud = LineGather(ud_v, zu_s.at[0], zu_r, zu_s.at[1], zu_s.at[2], clip, seq, 2)
    line_e = LineGather(e_v, ze_s.at[0], ze_r, ze_s.at[1], ze_s.at[2], clip, seq, 1)
    ud_wait.wait_recv()
    line_ud.step(0, 0)
    line_ud.step(0, 1)

    low = iota((ROWS, 1), 0) % 8
    for j in range(N):
        code = own64[:, j : j + 1] * CAP + j * 8 + low
        code_v[j * ROWS : (j + 1) * ROWS, :] = (
            (iota((ROWS, N * CAP), 1) == code).astype(F32).astype(BF16)
        )

    own_me = jnp.sum(
        jnp.where(iota((ROWS, N), 1) == seq, own64, 0), axis=1, keepdims=True
    )
    lane = iota((ROWS, N * 8), 1)
    gather = ((own_me == lane // 8) & (low == lane % 8)).astype(F32).astype(BF16)
    a2a_wait.wait_recv()
    arrived = jnp.concatenate([row_recv[d].astype(F32) for d in range(N)], axis=0).astype(BF16)
    rows_v[seq] = dot(gather, arrived, NN).astype(BF16)
    rows_ag = PlaneGather(rows_v, ag_s, ag_r, clip, seq, ((0, 16, 32), (32, 48, 64)))
    rows_ag.first()
    all_peers(e_copy)

    wide = jnp.concatenate([w_out[...].astype(F32), jnp.zeros((HPAD - HEAD, D), F32)], axis=0)
    wo_v[0, seq] = wide[:, :HALF].astype(BF16)
    wo_v[1, seq] = jnp.concatenate(
        [wide[:, HALF:], jnp.zeros((HPAD, 2 * HALF - D), F32)], axis=1
    ).astype(BF16)
    wo_ag = PlaneGather(wo_v.at[core], wo_s, wo_r, clip, seq, ((0, 32, 48), (48, 80, 96)))

    line_ud.step(1, 0)
    rows_ag.second()

    loads[1].wait()
    dec_masked = (mask_token[...].astype(F32).reshape(1, DEC) + pos_v[...].astype(F32)).astype(BF16)

    def mlp_start(dec_in, count):
        acc_v[0:count, :] = dec_in.astype(F32)
        dn_v[0:count, :] = norm_rows(dec_in.astype(F32), dec_gain[...].reshape(1, DEC))

    mlp_start(dec_masked, TOK)
    line_ud.step(1, 1)
    rows_ag.third()

    r256, c256 = iota((256, 256), 0), iota((256, 256), 1)
    unit = r256 % 128
    order_ud = (c256 == (unit // 8) * 16 + unit % 8 + 8 * (r256 // 128)).astype(F32).astype(BF16)
    r192, c192 = iota((192, 256), 0), iota((192, 256), 1)
    order_e = (c192 == (r192 % 32) * 8 + r192 // 32).astype(F32).astype(BF16)

    def sort_ud(b):
        two = dot(order_ud, ud_v[b], NN).astype(BF16)
        at = pl.ds(pl.multiple_of(b * 128, 128), 128)
        up_v[at, :] = two[:128]
        down_v[at, :] = two[128:]

    def sort_e(b):
        lines = dot(order_e, e_v[b], NN).astype(BF16)
        at = pl.ds(pl.multiple_of(b * 32, 32), 32)
        for q in range(6):
            emb_v[at, q * 256 : (q + 1) * 256] = lines[q * 32 : (q + 1) * 32]

    line_ud.step(2, 0)
    for t in (0, -1, 1):
        sort_ud(line_ud.block(t))
    rows_ag.relay(0)
    line_ud.step(2, 1)
    rows_ag.relay(-1)
    for t in (-2, 2):
        sort_ud(line_ud.block(t))
    line_ud.step(3, 0)
    rows_ag.relay(1)
    line_ud.step(3, 1)
    rows_ag.relay(2)
    wo_ag.first()
    for t in (-3, 3):
        sort_ud(line_ud.block(t))
    for p in (0, -1, 1, 2):
        rows_ag.last(p)
    line_ud.step(4, 0)
    line_ud.step(4, 1)
    e_wait.wait_recv()
    line_e.step(0)

    zeros_q = jnp.zeros((HPAD - HEAD, 256), F32)
    zeros_k = jnp.zeros((256, HPAD - HEAD), F32)

    def project(b):
        rows = rows_v[4 * b : 4 * b + 4].reshape(256, D)
        at = pl.ds(b * 256, 256)
        for i, top in ((0, 0), (2, HPAD)):
            part = dot(w_qkv[i], rows, NT)
            qv_v[pl.ds(top, HPAD), at] = jnp.concatenate([part, zeros_q], axis=0).astype(BF16)
        keys = dot(rows, w_qkv[1], NT)
        keys_v[at, :] = jnp.concatenate([keys, zeros_k], axis=1).astype(BF16)

    def attend(b):
        at = pl.ds(b * 256, 256)
        scores = dot(keys_v[...], qv_v[pl.ds(0, HPAD), at], NN)
        peak = jnp.max(scores, axis=0, keepdims=True)
        expo = jnp.exp2((scores - peak) * EXP_SCALE)
        total = jnp.sum(expo, axis=0, keepdims=True)
        probs = (expo * (1.0 / total)).astype(BF16)
        ho_v[:, at] = dot(qv_v[pl.ds(HPAD, HPAD), :], probs, NN).astype(BF16)

    project(0)
    project(1)
    wo_ag.second()
    project(2)
    project(3)
    wo_ag.third()
    attend(0)
    line_e.step(1)
    attend(1)
    wo_ag.relay(0)
    attend(2)
    wo_ag.relay(-1)
    attend(3)

    @pl.loop(0, N // 2, unroll=4)
    def _(h):
        two = dot(
            ho_v[...], code_v[:, pl.ds(pl.multiple_of(h * 256, 256), 256)], NN
        ).astype(BF16)
        ho_send[2 * h] = two[:, :CAP]
        ho_send[2 * h + 1] = two[:, CAP:]

    ho_recv[seq] = ho_send[seq]
    all_peers(ho_copy)
    line_e.step(2)
    sort_ud(line_ud.block(4))
    line_ud.sides()

    @pl.loop(0, 8, unroll=4)
    def _(t):
        sort_ud((other + 2 * t) % 16)

    def mlp(count):
        @pl.loop(0, 4, unroll=2)
        def _(h):
            at = pl.ds(pl.multiple_of(h * 512, 512), 512)
            hidden = jax.nn.gelu(dot(dn_v[0:count, :], up_v[at, :], NT)).astype(BF16)
            acc_v[0:count, :] += dot(hidden, down_v[at, :], NN)

        return acc_v[0:count, :].astype(BF16)

    dec_v[...] = mlp(TOK)
    line_e.step(3)
    wo_ag.relay(1)
    wo_ag.relay(2)
    loads[2].wait()
    loads[3].wait()
    keep = 1.0 - seen_v[...]

    x, y = seq // 4, seq % 4
    first_at, second_at = (x, y), (y, x)

    def plane_dev(fam, p, q):
        return (clip, p * 4 + q if fam == 0 else q * 4 + p)

    def g_first(fam, o):
        p, q = first_at[fam], second_at[fam]
        to = (p + o) % 4
        return rcopy(
            g_send.at[fam, pl.ds(to * 4, 4)],
            g_recv.at[fam, p],
            g_s.at[fam, 0],
            g_s.at[fam, 1],
            plane_dev(fam, to, q),
        )

    def g_second(fam, o):
        p, q = first_at[fam], second_at[fam]
        to = (q + o) % 4
        return rcopy(
            g_mid.at[fam, to],
            g_last.at[fam, q],
            g_s.at[fam, 2],
            g_s.at[fam, 3],
            plane_dev(fam, p, to),
        )

    for fam, (lo, hi) in enumerate(((0, 640), (640, PIX))):
        predicted = dot(pix_v[lo:hi, :], dec_v[...], NT)
        resid = ((predicted - tgt_v[lo:hi, :].astype(F32)) * keep).astype(BF16)
        for quarter in range(4):
            term = dot(dec_v[:, quarter * 128 : (quarter + 1) * 128], resid, TT) * (2.0 / PIX)
            if hi - lo < 640:
                term = jnp.concatenate([term, jnp.zeros((128, 640 - hi + lo), F32)], axis=1)
            for i in range(4):
                spot_g = quarter * 4 + i if fam == 0 else i * 4 + quarter
                g_send[fam, spot_g] = term[32 * i : 32 * i + 32].astype(BF16)
        for o in (1, 2, 3):
            g_first(fam, o).start()

    for p in (0, -1, 1, 2):
        wo_ag.last(p)

    def wo_side(j):
        ref = wo_v.at[core, j]
        return rcopy(ref, ref, wside_s.at[0], wside_s.at[1], (other, seq))

    wo_rest = wo_v.at[0, many]
    wo_wait = rcopy(wo_rest, wo_rest, wside_s.at[0], wside_s.at[1], (other, seq))
    all_peers(wo_side)
    line_e.step(4)
    line_e.sides()

    @pl.loop(0, N, unroll=4)
    def _(b):
        sort_e(b)

    pos_rows = dot(pick_v[...], pos_v[...], NN)

    ho_wait.wait_recv()
    wo_wait.wait_recv()
    heads = ho_recv[...].reshape(N * HPAD, CAP)
    attended = jnp.concatenate(
        [dot(heads, wo_v[half].reshape(N * HPAD, HALF), TN) for half in range(2)], axis=1
    )
    encoded = (visible_v[...] + attended[:, :D]).astype(BF16)
    embedded = dot(encoded, emb_v[:, :D], NT).astype(BF16)
    mlp_start((embedded.astype(F32) + pos_rows).astype(BF16), CAP)

    for fam in (0, 1):
        p, q = first_at[fam], second_at[fam]
        three = pl.ds(0, 3)
        rcopy(
            g_recv.at[fam, three], g_recv.at[fam, three], g_s.at[fam, 0], g_s.at[fam, 1], next_dev
        ).wait_recv()
        part = g_send[fam, pl.ds(p * 4, 4)].astype(F32)
        for o in (1, 2, 3):
            part = part + g_recv[fam, (p + o) % 4].astype(F32)
        g_mid[fam] = part.astype(BF16)
        for o in (1, 2, 3):
            g_second(fam, o).start()

    vis_dec = mlp(CAP)
    pick_dot = dot(pick_v[...], vis_dec, TN)
    seen_col = dot(pick_v[...], jnp.ones((CAP, DEC), BF16), TN)
    decoded_out[...] = jnp.where(seen_col > 0.5, pick_dot, dec_v[...].astype(F32)).astype(BF16)

    sums = []
    for fam in (0, 1):
        p, q = first_at[fam], second_at[fam]
        three = pl.ds(0, 3)
        rcopy(
            g_last.at[fam, three], g_last.at[fam, three], g_s.at[fam, 2], g_s.at[fam, 3], next_dev
        ).wait_recv()
        total = g_mid[fam, q].astype(F32)
        for o in (1, 2, 3):
            total = total + g_last[fam, (q + o) % 4].astype(F32)
        sums.append(total)
    grad_out[...] = jnp.concatenate(sums, axis=1)[:, :PIX]

    for made in (ud_wait, e_wait, a2a_wait, ho_wait, wo_wait):
        made.wait_send()
    for fam in (0, 1):
        three = pl.ds(0, 3)
        rcopy(
            g_recv.at[fam, three], g_recv.at[fam, three], g_s.at[fam, 0], g_s.at[fam, 1], next_dev
        ).wait_send()
        rcopy(
            g_last.at[fam, three], g_last.at[fam, three], g_s.at[fam, 2], g_s.at[fam, 3], next_dev
        ).wait_send()
    rows_ag.finish()
    wo_ag.finish()
    line_ud.finish()
    line_e.finish()


def shards(
    patches,
    vis_index,
    enc_gain,
    w_qkv,
    w_out,
    w_embed,
    mask_token,
    pos_embed,
    dec_gain,
    w_up,
    w_down,
    w_pixel,
    target,
):
    vmem = pl.BlockSpec(memory_space=pltpu.VMEM)
    hbm = pl.BlockSpec(memory_space=pl.ANY)
    dma = pltpu.SemaphoreType.DMA
    decoded, grad = pl.pallas_call(
        kernel,
        out_shape=(
            jax.ShapeDtypeStruct((TOK, DEC), BF16),
            jax.ShapeDtypeStruct((DEC // N, PIX), F32),
        ),
        in_specs=[hbm, vmem, vmem, vmem, vmem, vmem, vmem, hbm, vmem, vmem, vmem, hbm, hbm],
        out_specs=(vmem, vmem),
        scratch_shapes=[
            pltpu.VMEM((TOK, D), BF16),
            pltpu.VMEM((TOK, DEC), BF16),
            pltpu.VMEM((PIX, DEC), BF16),
            pltpu.VMEM((PIX, TOK), BF16),
            pltpu.VMEM((16, 512), BF16),
            pltpu.VMEM((16, 256), BF16),
            pltpu.VMEM((CAP, TOK), BF16),
            pltpu.VMEM((1, TOK), F32),
            pltpu.VMEM((CAP, D), F32),
            pltpu.VMEM((N, 8, D), BF16),
            pltpu.VMEM((N, 8, D), BF16),
            pltpu.VMEM((N, ROWS, D), BF16),
            pltpu.VMEM((VIS, N * CAP), BF16),
            pltpu.VMEM((2 * HPAD, VIS), BF16),
            pltpu.VMEM((VIS, HPAD), BF16),
            pltpu.VMEM((HPAD, VIS), BF16),
            pltpu.VMEM((N, HPAD, CAP), BF16),
            pltpu.VMEM((N, HPAD, CAP), BF16),
            pltpu.VMEM((2, N, HPAD, HALF), BF16),
            pltpu.VMEM((N, 256, 512), BF16),
            pltpu.VMEM((N, 256, 256), BF16),
            pltpu.VMEM((HID, DEC), BF16),
            pltpu.VMEM((HID, DEC), BF16),
            pltpu.VMEM((DEC, 2 * HALF), BF16),
            pltpu.VMEM((TOK, DEC), F32),
            pltpu.VMEM((TOK, DEC), BF16),
            pltpu.VMEM((TOK, DEC), BF16),
            pltpu.VMEM((2, N, 32, 640), BF16),
            pltpu.VMEM((2, 4, 4, 32, 640), BF16),
            pltpu.VMEM((2, 4, 32, 640), BF16),
            pltpu.VMEM((2, 4, 32, 640), BF16),
            dma((4,)),
            dma((2,)),
            dma((2,)),
            dma((2,)),
            dma((2,)),
            dma((2, 4)),
            dma((2,)),
            dma,
            dma((10,)),
            dma,
            dma((10,)),
            dma((3,)),
            dma((8,)),
            dma((3,)),
            dma((4,)),
        ],
        compiler_params=pltpu.CompilerParams(
            collective_id=0, has_side_effects=True, vmem_limit_bytes=60 * 1024 * 1024
        ),
    )(
        patches[0],
        vis_index,
        enc_gain,
        jnp.transpose(w_qkv, (0, 2, 1)),
        w_out,
        w_embed.T,
        mask_token,
        pos_embed,
        dec_gain,
        w_up.T,
        w_down,
        w_pixel.T,
        target[0].T,
    )
    return decoded[None], grad[None]


def solution(mesh):
    placed = (
        P("clip", "seq", None),
        P("clip", None),
        P(),
        P(None, None, "seq"),
        P("seq", None),
        P(None, ("clip", "seq")),
        P(),
        P("seq", None),
        P(),
        P(None, ("clip", "seq")),
        P(("clip", "seq"), None),
        P(),
        P("clip", "seq", None),
    )
    return jax.shard_map(
        shards,
        mesh=mesh,
        in_specs=placed,
        out_specs=(P("clip", "seq", None), P("clip", "seq", None)),
        check_vma=False,
    )
```

```python
import jax
import jax.numpy as jnp
from jax import lax
from jax.experimental import pallas as pl
from jax.experimental.pallas import tpu as pltpu
from jax.sharding import PartitionSpec as P

D = 1408
HEAD = 88
HPAD = 96
DEC = 512
HID = 2048
PIX = 1176
TOK = 640
CAP = 128
VIS = 1024
N = 16
ROWS = VIS // N
HALF = 768
F32 = jnp.float32
BF16 = jnp.bfloat16
MESH = pl.DeviceIdType.MESH
EXP_SCALE = HEAD ** (-0.5) * 1.4426950408889634

NT = (((1,), (1,)), ((), ()))
NN = (((1,), (0,)), ((), ()))
TN = (((0,), (0,)), ((), ()))
TT = (((0,), (1,)), ((), ()))


def dot(left, right, dims):
    return lax.dot_general(left, right, dims, preferred_element_type=F32)


def iota(shape, axis):
    return lax.broadcasted_iota(jnp.int32, shape, axis)


def norm_rows(values, gain):
    center = jnp.mean(values, axis=-1, keepdims=True)
    spread = jnp.mean((values - center) ** 2, axis=-1, keepdims=True)
    return ((values - center) * lax.rsqrt(spread + 1e-05) * gain).astype(BF16)


def rcopy(src, dst, send_sem, recv_sem, dev):
    return pltpu.make_async_remote_copy(
        src_ref=src,
        dst_ref=dst,
        send_sem=send_sem,
        recv_sem=recv_sem,
        device_id=dev,
        device_id_type=MESH,
    )


class PlaneGather:
    def __init__(self, buf, send, recv, clip, seq, cuts):
        self.buf, self.send, self.recv, self.clip = buf, send, recv, clip
        self.x, self.y = seq // 4, seq % 4
        self.cuts = cuts

    def rank(self, fam, p, q):
        dx, dy = (p, q) if fam == 0 else (q, p)
        return ((self.x + dx + 4) % 4) * 4 + (self.y + dy + 4) % 4

    def piece(self, fam, p, q, part):
        lo, mid, hi = self.cuts[fam]
        lo, hi = ((lo, hi), (lo, mid), (mid, hi))[part]
        return self.buf.at[self.rank(fam, p, q), pl.ds(lo, hi - lo)]

    def go(self, fam, p, q, part, to, stage):
        ref = self.piece(fam, p, q, part)
        dev = (self.clip, self.rank(fam, *to))
        rcopy(ref, ref, self.send, self.recv.at[stage], dev).start()

    def got(self, stage, pieces):
        ref = self.buf.at[pl.ds(0, pieces)]
        rcopy(ref, ref, self.send, self.recv.at[stage], (self.clip, self.rank(0, 1, 0))).wait_recv()

    def spread(self, fam, p):
        self.go(fam, p, 0, 0, (0, 1), 2 + p % 4)
        self.go(fam, p, 0, 0, (0, -1), 2 + p % 4)

    def first(self):
        for fam in (0, 1):
            self.go(fam, 0, 0, 0, (1, 0), 0)
            self.go(fam, 0, 0, 0, (-1, 0), 0)
        for fam in (0, 1):
            self.spread(fam, 0)

    def second(self):
        self.got(0, 2)
        for fam in (0, 1):
            self.go(fam, -1, 0, 1, (1, 0), 1)
            self.go(fam, 1, 0, 2, (-1, 0), 1)
        for fam in (0, 1):
            self.spread(fam, -1)
            self.spread(fam, 1)

    def third(self):
        self.got(1, 1)
        for fam in (0, 1):
            self.spread(fam, 2)

    def relay(self, p):
        self.got(2 + p % 4, 2)
        for fam in (0, 1):
            self.go(fam, p, -1, 1, (0, 1), 6 + p % 4)
            self.go(fam, p, 1, 2, (0, -1), 6 + p % 4)

    def last(self, p):
        self.got(6 + p % 4, 1)

    def finish(self):
        ref = self.buf.at[pl.ds(0, N - 1)]
        rcopy(ref, ref, self.send, self.recv.at[0], (self.clip, self.rank(0, 1, 0))).wait_send()


class LineGather:
    def __init__(self, buf, send, recv, side_send, side_recv, clip, seq, subs):
        self.buf, self.send, self.recv = buf, send, recv
        self.side_send, self.side_recv = side_send, side_recv
        self.clip, self.seq, self.subs = clip, seq, subs
        self.other = clip + 1 - 2 * (clip % 2)
        self.rows = buf.shape[1]

    def block(self, step):
        return (self.clip + 2 * step + 16) % 16

    def go(self, step, lo, size, way, sem):
        ref = self.buf.at[self.block(step), pl.ds(lo, size)]
        rcopy(ref, ref, self.send, self.recv.at[sem], (self.block(way), self.seq)).start()

    def got(self, sem, rows):
        ref = self.buf.at[0, pl.ds(0, rows)]
        rcopy(ref, ref, self.send, self.recv.at[sem], (self.block(1), self.seq)).wait_recv()

    def side(self, step):
        ref = self.buf.at[self.block(step)]
        rcopy(ref, ref, self.side_send, self.side_recv, (self.other, self.seq)).start()

    def step(self, t, sub=0):
        size = self.rows // self.subs
        sem = t * self.subs + sub
        half = self.rows // 2
        done = sub == self.subs - 1
        if t == 0:
            self.go(0, sub * size, size, 1, sem)
            self.go(0, sub * size, size, -1, sem)
            if done:
                self.side(0)
        elif t == 4:
            self.got(sem - self.subs, half if self.subs == 2 else self.rows)
            if done:
                self.side(4)
        else:
            both = self.buf.at[pl.ds(0, 2), pl.ds(0, size)]
            rcopy(
                both, both, self.send, self.recv.at[sem - self.subs], (self.block(1), self.seq)
            ).wait_recv()
            if t < 3:
                self.go(-t, sub * size, size, 1, sem)
                self.go(t, sub * size, size, -1, sem)
            else:
                if sub == 0:
                    self.go(-3, 0, half, 1, sem)
                if done:
                    self.go(3, half, half, -1, sem)
            if done:
                self.side(-t)
                self.side(t)

    def sides(self):
        ref = self.buf.at[pl.ds(0, 8)]
        rcopy(ref, ref, self.side_send, self.side_recv, (self.other, self.seq)).wait_recv()

    def finish(self):
        ref = self.buf.at[pl.ds(0, 7)]
        rcopy(ref, ref, self.send, self.recv.at[0], (self.block(1), self.seq)).wait_send()
        ref = self.buf.at[pl.ds(0, 8)]
        rcopy(ref, ref, self.side_send, self.side_recv, (self.other, self.seq)).wait_send()


def kernel(
    patches,
    vis,
    enc_gain,
    w_qkv,
    w_out,
    w_embed,
    mask_token,
    pos_embed,
    dec_gain,
    w_up,
    w_down,
    w_pixel,
    target,
    dec_out,
    vis_out,
    pick_out,
    sum_out,
    patch_v,
    pos_v,
    pix_v,
    tgt_v,
    ud_mine,
    e_mine,
    pick_v,
    seen_v,
    visible_v,
    row_send,
    row_recv,
    rows_v,
    code_v,
    qv_v,
    keys_v,
    ho_v,
    ho_send,
    ho_recv,
    wo_v,
    ud_v,
    e_v,
    up_v,
    down_v,
    emb_v,
    acc_v,
    dec_v,
    dn_v,
    g_send,
    g_recv,
    g_mid,
    g_last,
    load_sem,
    ud_s,
    e_s,
    a2a_s,
    ho_s,
    g_s,
    wside_s,
    ag_s,
    ag_r,
    wo_s,
    wo_r,
    zu_s,
    zu_r,
    ze_s,
    ze_r,
):
    clip, seq = lax.axis_index("clip"), lax.axis_index("seq")
    core = clip % 2
    other = clip + 1 - 2 * core

    loads = [
        pltpu.make_async_copy(src, dst, load_sem.at[i])
        for i, (src, dst) in enumerate(
            ((patches, patch_v), (pos_embed, pos_v), (w_pixel, pix_v), (target, tgt_v))
        )
    ]
    for load in loads:
        load.start()

    barrier = pltpu.get_barrier_semaphore()

    @pl.loop(1, N)
    def _(o):
        pl.semaphore_signal(
            barrier, inc=1, device_id=(clip, (seq + o) % N), device_id_type=MESH
        )

    for dev in (other, (clip + 2) % 16, (clip + 14) % 16):
        pl.semaphore_signal(barrier, inc=1, device_id=(dev, seq), device_id_type=MESH)

    ud_mine[...] = jnp.concatenate(
        [w_up[...].astype(F32), w_down[...].astype(F32)], axis=0
    ).astype(BF16)
    emb_rows = jnp.concatenate([w_embed[...].astype(F32), jnp.zeros((2, 128), F32)], axis=1)
    packed = jnp.zeros((16, 256), F32)
    row16 = iota((16, 256), 0)
    for a in range(2):
        for q in range(6):
            line = jnp.broadcast_to(emb_rows[a : a + 1, q * 256 : (q + 1) * 256], (16, 256))
            packed = jnp.where(row16 == a * 8 + q, line, packed)
    e_mine[...] = packed.astype(BF16)
    my16 = pl.ds(pl.multiple_of(seq * 16, 16), 16)
    ud_v[clip, my16, :] = ud_mine[...]
    e_v[clip, my16, :] = e_mine[...]

    def all_peers(copy):
        @pl.loop(1, N)
        def _(o):
            copy((seq + o) % N).start()

    next_dev = (clip, (seq + 1) % N)

    def both(src, dst, sems):
        return rcopy(src, dst, sems.at[0], sems.at[1], next_dev)

    def ud_copy(peer):
        return rcopy(ud_mine, ud_v.at[clip, my16], ud_s.at[0], ud_s.at[1], (clip, peer))

    def e_copy(peer):
        return rcopy(e_mine, e_v.at[clip, my16], e_s.at[0], e_s.at[1], (clip, peer))

    def a2a_copy(peer):
        return rcopy(row_send.at[peer], row_recv.at[seq], a2a_s.at[0], a2a_s.at[1], (clip, peer))

    def ho_copy(peer):
        return rcopy(ho_send.at[peer], ho_recv.at[seq], ho_s.at[0], ho_s.at[1], (clip, peer))

    many = pl.ds(0, N - 1)
    ud_all = ud_v.at[clip, pl.ds(0, 16 * (N - 1))]
    e_all = e_v.at[clip, pl.ds(0, 16 * (N - 1))]
    ud_wait = both(ud_all, ud_all, ud_s)
    e_wait = both(e_all, e_all, e_s)
    a2a_wait = both(row_send.at[many], row_recv.at[many], a2a_s)
    ho_wait = both(ho_send.at[many], ho_recv.at[many], ho_s)

    token = vis[...]
    here = iota((ROWS, VIS), 1) // N == iota((ROWS, VIS), 0)
    column = (iota((VIS, N), 0) % N == iota((VIS, N), 1)).astype(F32).astype(BF16)

    def digit(values):
        spread = jnp.where(here, jnp.broadcast_to(values, (ROWS, VIS)), 0)
        return dot(spread.astype(F32).astype(BF16), column, NN)

    v64 = (digit(token // 128) * 128.0 + digit(token % 128)).astype(jnp.int32)
    own64 = jnp.zeros((ROWS, N), jnp.int32)
    for d in range(1, N):
        own64 = own64 + (v64 >= d * TOK).astype(jnp.int32)
    mine = jnp.where(own64 == seq, v64 - seq * TOK + 1, 0)
    place = mine[0:8]
    for a in range(1, 8):
        place = place + mine[8 * a : 8 * a + 8]
    spot = jnp.concatenate([place[:, j : j + 1] for j in range(N)], axis=0) - 1
    pick = (iota((CAP, TOK), 1) == spot).astype(F32)
    seen_v[...] = jnp.sum(pick, axis=0, keepdims=True)
    pick_v[...] = pick.astype(BF16)
    loads[0].wait()
    visible = dot(pick_v[...], patch_v[...], NN)
    visible_v[...] = visible
    center = jnp.mean(visible, axis=-1, keepdims=True)
    spread = jnp.mean((visible - center) ** 2, axis=-1, keepdims=True)
    normed = (visible - center) * lax.rsqrt(spread + 1e-05) * enc_gain[...].reshape(1, D)
    for j in range(N):
        row_send[j] = normed[8 * j : 8 * j + 8].astype(BF16)
    row_recv[seq] = row_send[seq]

    wide = jnp.concatenate([w_out[...].astype(F32), jnp.zeros((HPAD - HEAD, D), F32)], axis=0)
    wo_v[0, seq] = wide[:, :HALF].astype(BF16)
    wo_v[1, seq] = jnp.concatenate(
        [wide[:, HALF:], jnp.zeros((HPAD, 2 * HALF - D), F32)], axis=1
    ).astype(BF16)
    wo_ag = PlaneGather(wo_v.at[core], wo_s, wo_r, clip, seq, ((0, 32, 48), (48, 80, 96)))

    pl.semaphore_wait(barrier, N - 1 + 3)
    all_peers(ud_copy)
    all_peers(a2a_copy)
    wo_ag.first()

    line_ud = LineGather(ud_v, zu_s.at[0], zu_r, zu_s.at[1], zu_s.at[2], clip, seq, 2)
    line_e = LineGather(e_v, ze_s.at[0], ze_r, ze_s.at[1], ze_s.at[2], clip, seq, 1)
    ud_wait.wait_recv()
    line_ud.step(0, 0)
    line_ud.step(0, 1)

    low = iota((ROWS, 1), 0) % 8
    for j in range(N):
        code = own64[:, j : j + 1] * CAP + j * 8 + low
        code_v[j * ROWS : (j + 1) * ROWS, :] = (
            (iota((ROWS, N * CAP), 1) == code).astype(F32).astype(BF16)
        )

    own_me = jnp.sum(
        jnp.where(iota((ROWS, N), 1) == seq, own64, 0), axis=1, keepdims=True
    )
    lane = iota((ROWS, N * 8), 1)
    gather = ((own_me == lane // 8) & (low == lane % 8)).astype(F32).astype(BF16)
    a2a_wait.wait_recv()
    arrived = jnp.concatenate([row_recv[d].astype(F32) for d in range(N)], axis=0).astype(BF16)
    rows_v[seq] = dot(gather, arrived, NN).astype(BF16)
    rows_ag = PlaneGather(rows_v, ag_s, ag_r, clip, seq, ((0, 16, 32), (32, 48, 64)))
    rows_ag.first()

    line_ud.step(1, 0)
    rows_ag.second()

    loads[1].wait()
    dec_masked = (mask_token[...].astype(F32).reshape(1, DEC) + pos_v[...].astype(F32)).astype(BF16)

    def mlp_start(dec_in, count):
        acc_v[0:count, :] = dec_in.astype(F32)
        dn_v[0:count, :] = norm_rows(dec_in.astype(F32), dec_gain[...].reshape(1, DEC))

    mlp_start(dec_masked, TOK)
    line_ud.step(1, 1)
    rows_ag.third()

    r256, c256 = iota((256, 256), 0), iota((256, 256), 1)
    unit = r256 % 128
    order_ud = (c256 == (unit // 8) * 16 + unit % 8 + 8 * (r256 // 128)).astype(F32).astype(BF16)
    r192, c192 = iota((192, 256), 0), iota((192, 256), 1)
    order_e = (c192 == (r192 % 32) * 8 + r192 // 32).astype(F32).astype(BF16)

    def sort_ud(b):
        two = dot(order_ud, ud_v[b], NN).astype(BF16)
        at = pl.ds(pl.multiple_of(b * 128, 128), 128)
        up_v[at, :] = two[:128]
        down_v[at, :] = two[128:]

    def sort_e(b):
        lines = dot(order_e, e_v[b], NN).astype(BF16)
        at = pl.ds(pl.multiple_of(b * 32, 32), 32)
        for q in range(6):
            emb_v[at, q * 256 : (q + 1) * 256] = lines[q * 32 : (q + 1) * 32]

    line_ud.step(2, 0)
    for t in (0, -1, 1):
        sort_ud(line_ud.block(t))
    wo_ag.second()
    rows_ag.relay(0)
    line_ud.step(2, 1)
    rows_ag.relay(-1)
    wo_ag.third()
    for t in (-2, 2):
        sort_ud(line_ud.block(t))
    line_ud.step(3, 0)
    rows_ag.relay(1)
    line_ud.step(3, 1)
    rows_ag.relay(2)
    all_peers(e_copy)
    for t in (-3, 3):
        sort_ud(line_ud.block(t))
    for p in (0, -1, 1, 2):
        rows_ag.last(p)

    zeros_q = jnp.zeros((HPAD - HEAD, 256), F32)
    zeros_k = jnp.zeros((256, HPAD - HEAD), F32)

    def project(b):
        rows = rows_v[4 * b : 4 * b + 4].reshape(256, D)
        at = pl.ds(b * 256, 256)
        for i, top in ((0, 0), (2, HPAD)):
            part = dot(w_qkv[i], rows, NT)
            qv_v[pl.ds(top, HPAD), at] = jnp.concatenate([part, zeros_q], axis=0).astype(BF16)
        keys = dot(rows, w_qkv[1], NT)
        keys_v[at, :] = jnp.concatenate([keys, zeros_k], axis=1).astype(BF16)

    def attend(b):
        at = pl.ds(b * 256, 256)
        scores = dot(keys_v[...], qv_v[pl.ds(0, HPAD), at], NN)
        peak = jnp.max(scores, axis=0, keepdims=True)
        expo = jnp.exp2((scores - peak) * EXP_SCALE)
        total = jnp.sum(expo, axis=0, keepdims=True)
        probs = (expo * (1.0 / total)).astype(BF16)
        ho_v[:, at] = dot(qv_v[pl.ds(HPAD, HPAD), :], probs, NN).astype(BF16)

    project(0)
    line_ud.step(4, 0)
    wo_ag.relay(0)
    project(1)
    line_ud.step(4, 1)
    e_wait.wait_recv()
    line_e.step(0)
    project(2)
    wo_ag.relay(-1)
    project(3)
    sort_ud(line_ud.block(4))
    line_ud.sides()

    @pl.loop(0, 8, unroll=4)
    def _(t):
        sort_ud((other + 2 * t) % 16)

    def mlp_part(count, h):
        at = pl.ds(h * 512, 512)
        hidden = jax.nn.gelu(dot(dn_v[0:count, :], up_v[at, :], NT)).astype(BF16)
        acc_v[0:count, :] += dot(hidden, down_v[at, :], NN)

    mlp_part(TOK, 0)
    wo_ag.relay(1)
    mlp_part(TOK, 1)
    mlp_part(TOK, 2)
    wo_ag.relay(2)
    mlp_part(TOK, 3)
    dec_v[...] = acc_v[...].astype(BF16)
    line_e.step(1)
    loads[2].wait()
    loads[3].wait()
    keep = 1.0 - seen_v[...]

    x, y = seq // 4, seq % 4
    first_at, second_at = (x, y), (y, x)

    def plane_dev(fam, p, q):
        return (clip, p * 4 + q if fam == 0 else q * 4 + p)

    def g_first(fam, o):
        p, q = first_at[fam], second_at[fam]
        to = (p + o) % 4
        return rcopy(
            g_send.at[fam, pl.ds(to * 4, 4)],
            g_recv.at[fam, p],
            g_s.at[fam, 0],
            g_s.at[fam, 1],
            plane_dev(fam, to, q),
        )

    def g_second(fam, o):
        p, q = first_at[fam], second_at[fam]
        to = (q + o) % 4
        return rcopy(
            g_mid.at[fam, to],
            g_last.at[fam, q],
            g_s.at[fam, 2],
            g_s.at[fam, 3],
            plane_dev(fam, p, to),
        )

    for fam, (lo, hi) in enumerate(((0, 640), (640, PIX))):
        predicted = dot(pix_v[lo:hi, :], dec_v[...], NT)
        resid = ((predicted - tgt_v[lo:hi, :].astype(F32)) * keep).astype(BF16)
        for quarter in range(4):
            term = dot(dec_v[:, quarter * 128 : (quarter + 1) * 128], resid, TT) * (2.0 / PIX)
            if hi - lo < 640:
                term = jnp.concatenate([term, jnp.zeros((128, 640 - hi + lo), F32)], axis=1)
            for i in range(4):
                spot_g = quarter * 4 + i if fam == 0 else i * 4 + quarter
                g_send[fam, spot_g] = term[32 * i : 32 * i + 32].astype(BF16)
        for o in (1, 2, 3):
            g_first(fam, o).start()

    line_e.step(2)
    for p in (0, -1, 1, 2):
        wo_ag.last(p)

    def wo_side(j):
        ref = wo_v.at[core, j]
        return rcopy(ref, ref, wside_s.at[0], wside_s.at[1], (other, seq))

    wo_rest = wo_v.at[0, many]
    wo_wait = rcopy(wo_rest, wo_rest, wside_s.at[0], wside_s.at[1], (other, seq))
    all_peers(wo_side)
    attend(0)
    attend(1)
    line_e.step(3)
    attend(2)
    attend(3)

    @pl.loop(0, N // 2, unroll=4)
    def _(h):
        two = dot(
            ho_v[...], code_v[:, pl.ds(pl.multiple_of(h * 256, 256), 256)], NN
        ).astype(BF16)
        ho_send[2 * h] = two[:, :CAP]
        ho_send[2 * h + 1] = two[:, CAP:]

    ho_recv[seq] = ho_send[seq]
    all_peers(ho_copy)
    line_e.step(4)
    for fam in (0, 1):
        p, q = first_at[fam], second_at[fam]
        three = pl.ds(0, 3)
        rcopy(
            g_recv.at[fam, three], g_recv.at[fam, three], g_s.at[fam, 0], g_s.at[fam, 1], next_dev
        ).wait_recv()
        part = g_send[fam, pl.ds(p * 4, 4)].astype(F32)
        for o in (1, 2, 3):
            part = part + g_recv[fam, (p + o) % 4].astype(F32)
        g_mid[fam] = part.astype(BF16)
        for o in (1, 2, 3):
            g_second(fam, o).start()

    line_e.sides()

    @pl.loop(0, N, unroll=4)
    def _(b):
        sort_e(b)

    pos_rows = dot(pick_v[...], pos_v[...], NN)

    ho_wait.wait_recv()
    wo_wait.wait_recv()
    heads = ho_recv[...].reshape(N * HPAD, CAP)
    attended = jnp.concatenate(
        [dot(heads, wo_v[half].reshape(N * HPAD, HALF), TN) for half in range(2)], axis=1
    )
    encoded = (visible_v[...] + attended[:, :D]).astype(BF16)
    embedded = dot(encoded, emb_v[:, :D], NT).astype(BF16)
    mlp_start((embedded.astype(F32) + pos_rows).astype(BF16), CAP)

    for h in range(4):
        mlp_part(CAP, h)
    vis_dec = acc_v[0:CAP, :].astype(BF16)
    dec_out[...] = dec_v[...]
    vis_out[...] = vis_dec
    pick_out[...] = pick_v[...]

    sums = []
    for fam in (0, 1):
        p, q = first_at[fam], second_at[fam]
        three = pl.ds(0, 3)
        rcopy(
            g_last.at[fam, three], g_last.at[fam, three], g_s.at[fam, 2], g_s.at[fam, 3], next_dev
        ).wait_recv()
        total = g_mid[fam, q].astype(F32)
        for o in (1, 2, 3):
            total = total + g_last[fam, (q + o) % 4].astype(F32)
        sums.append(total)
    sum_out[...] = jnp.concatenate(sums, axis=1)[:, :PIX]

    for made in (ud_wait, e_wait, a2a_wait, ho_wait, wo_wait):
        made.wait_send()
    for fam in (0, 1):
        three = pl.ds(0, 3)
        rcopy(
            g_recv.at[fam, three], g_recv.at[fam, three], g_s.at[fam, 0], g_s.at[fam, 1], next_dev
        ).wait_send()
        rcopy(
            g_last.at[fam, three], g_last.at[fam, three], g_s.at[fam, 2], g_s.at[fam, 3], next_dev
        ).wait_send()
    rows_ag.finish()
    wo_ag.finish()
    line_ud.finish()
    line_e.finish()


def merge(
    dec_in, vis_in, pick_in, total_in, decoded_out, grad_out, dec, vis_dec, pick, total, sems
):
    moves = [
        pltpu.make_async_copy(src, dst, sems.at[i])
        for i, (src, dst) in enumerate(
            ((pick_in, pick), (vis_in, vis_dec), (dec_in, dec), (total_in, total))
        )
    ]
    for move in moves:
        move.start()
    for move in moves:
        move.wait()
    placed = dot(pick[...], vis_dec[...], TN)
    seen = dot(pick[...], jnp.ones((CAP, 128), BF16), TN)
    for lane in range(0, DEC, 128):
        at = slice(lane, lane + 128)
        old = dec[:, at].astype(F32)
        decoded_out[:, at] = jnp.where(seen > 0.5, placed[:, at], old).astype(BF16)
    grad_out[...] = total[...]


def shards(
    patches,
    vis_index,
    enc_gain,
    w_qkv,
    w_out,
    w_embed,
    mask_token,
    pos_embed,
    dec_gain,
    w_up,
    w_down,
    w_pixel,
    target,
):
    vmem = pl.BlockSpec(memory_space=pltpu.VMEM)
    hbm = pl.BlockSpec(memory_space=pl.ANY)
    dma = pltpu.SemaphoreType.DMA
    parts = pl.pallas_call(
        kernel,
        out_shape=(
            jax.ShapeDtypeStruct((TOK, DEC), BF16),
            jax.ShapeDtypeStruct((CAP, DEC), BF16),
            jax.ShapeDtypeStruct((CAP, TOK), BF16),
            jax.ShapeDtypeStruct((DEC // N, PIX), F32),
        ),
        in_specs=[hbm, vmem, vmem, vmem, vmem, vmem, vmem, hbm, vmem, vmem, vmem, hbm, hbm],
        out_specs=(vmem, vmem, vmem, vmem),
        scratch_shapes=[
            pltpu.VMEM((TOK, D), BF16),
            pltpu.VMEM((TOK, DEC), BF16),
            pltpu.VMEM((PIX, DEC), BF16),
            pltpu.VMEM((PIX, TOK), BF16),
            pltpu.VMEM((16, 512), BF16),
            pltpu.VMEM((16, 256), BF16),
            pltpu.VMEM((CAP, TOK), BF16),
            pltpu.VMEM((1, TOK), F32),
            pltpu.VMEM((CAP, D), F32),
            pltpu.VMEM((N, 8, D), BF16),
            pltpu.VMEM((N, 8, D), BF16),
            pltpu.VMEM((N, ROWS, D), BF16),
            pltpu.VMEM((VIS, N * CAP), BF16),
            pltpu.VMEM((2 * HPAD, VIS), BF16),
            pltpu.VMEM((VIS, HPAD), BF16),
            pltpu.VMEM((HPAD, VIS), BF16),
            pltpu.VMEM((N, HPAD, CAP), BF16),
            pltpu.VMEM((N, HPAD, CAP), BF16),
            pltpu.VMEM((2, N, HPAD, HALF), BF16),
            pltpu.VMEM((N, 256, 512), BF16),
            pltpu.VMEM((N, 256, 256), BF16),
            pltpu.VMEM((HID, DEC), BF16),
            pltpu.VMEM((HID, DEC), BF16),
            pltpu.VMEM((DEC, 2 * HALF), BF16),
            pltpu.VMEM((TOK, DEC), F32),
            pltpu.VMEM((TOK, DEC), BF16),
            pltpu.VMEM((TOK, DEC), BF16),
            pltpu.VMEM((2, N, 32, 640), BF16),
            pltpu.VMEM((2, 4, 4, 32, 640), BF16),
            pltpu.VMEM((2, 4, 32, 640), BF16),
            pltpu.VMEM((2, 4, 32, 640), BF16),
            dma((4,)),
            dma((2,)),
            dma((2,)),
            dma((2,)),
            dma((2,)),
            dma((2, 4)),
            dma((2,)),
            dma,
            dma((10,)),
            dma,
            dma((10,)),
            dma((3,)),
            dma((8,)),
            dma((3,)),
            dma((4,)),
        ],
        compiler_params=pltpu.CompilerParams(
            collective_id=0, has_side_effects=True, vmem_limit_bytes=60 * 1024 * 1024
        ),
    )(
        patches[0],
        vis_index,
        enc_gain,
        jnp.transpose(w_qkv, (0, 2, 1)),
        w_out,
        w_embed.T,
        mask_token,
        pos_embed,
        dec_gain,
        w_up.T,
        w_down,
        w_pixel.T,
        target[0].T,
    )
    decoded, grad = pl.pallas_call(
        merge,
        out_shape=(
            jax.ShapeDtypeStruct((TOK, DEC), BF16),
            jax.ShapeDtypeStruct((DEC // N, PIX), F32),
        ),
        in_specs=[hbm] * 4,
        out_specs=(vmem, vmem),
        scratch_shapes=[
            pltpu.VMEM((TOK, DEC), BF16),
            pltpu.VMEM((CAP, DEC), BF16),
            pltpu.VMEM((CAP, TOK), BF16),
            pltpu.VMEM((DEC // N, PIX), F32),
            dma((4,)),
        ],
        compiler_params=pltpu.CompilerParams(vmem_limit_bytes=60 * 1024 * 1024),
    )(*parts)
    return decoded[None], grad[None]


def solution(mesh):
    placed = (
        P("clip", "seq", None),
        P("clip", None),
        P(),
        P(None, None, "seq"),
        P("seq", None),
        P(None, ("clip", "seq")),
        P(),
        P("seq", None),
        P(),
        P(None, ("clip", "seq")),
        P(("clip", "seq"), None),
        P(),
        P("clip", "seq", None),
    )
    return jax.shard_map(
        shards,
        mesh=mesh,
        in_specs=placed,
        out_specs=(P("clip", "seq", None), P("clip", "seq", None)),
        check_vma=False,
    )
```
